32 devices in a mesh: groups: 2 (over x), side: 2 (over core), dev: 8 (over z, y).
Axes of the slice: x: 2, y: 2, z: 4, core: 2. Of those that a mesh axis runs over, the one named last changes fastest.
Arguments:
- queries: bfloat16 [256, 8192], P(('groups', 'side', 'dev')), parts along dimension 0, may hold values from -7 to 7
- kv_cache: bfloat16 [1408, 16, 1024], P(('groups', 'side', 'dev')), parts along dimension 0, may hold values from -6 to 6
- new_kv: bfloat16 [256, 1024], P(('groups', 'side', 'dev')), parts along dimension 0, may hold values from -6 to 6
- lengths: int32 [256], P(('groups', 'side', 'dev')), parts along dimension 0, may hold values from 1 to 256, as said below
- page_table: int32 [256, 16], P(('groups', 'side', 'dev')), parts along dimension 0, may hold values from 0 to 43, as said below
- hidden: bfloat16 [256, 4096], P(('groups', 'side', 'dev')), parts along dimension 0, may hold values from -6 to 6
- norm_gain: float32 [4096], replicated, may hold values from 0.5 to 1.5
- route_ids: int32 [256, 8], P(('groups', 'side', 'dev')), parts along dimension 0, may hold values from 0 to 31, all different within a row; in each aligned block of 8 rows (0 to 7, 8 to 15, ...) at most 4 rows name the same one
- route_weights: float32 [256, 8], P(('groups', 'side', 'dev')), parts along dimension 0, may hold values from 0.05 to 1
- gate_w: bfloat16 [4096, 49152], P(None, ('side', 'dev')), may hold values from -0.09375 to 0.09375
- up_w: bfloat16 [4096, 49152], P(None, ('side', 'dev')), may hold values from -0.09375 to 0.09375
- down_w: bfloat16 [49152, 4096], P(('side', 'dev')), may hold values from -0.15625 to 0.15625
Outputs:
- context: bfloat16 [256, 8192], P(('groups', 'side', 'dev')), parts along dimension 0
- moe_out: bfloat16 [256, 4096], P(('groups', 'side', 'dev')), parts along dimension 0
The draws below stay inside these ranges and needn't reach their ends.
There are 2 independent parts, one for each index of `groups`. The reference program is written for one: setup_inputs(seed, part) draws one part's arguments, and reference() takes and returns one part's arrays. A program takes and returns all parts, laid end to end along the dimension named above; an argument that names none is the same for every part. Nothing has to cross between parts.
Inputs may be any that keep to these rules, and one draw needn't show every extreme that they name: `route_ids`: within the rows of one device, no expert is named by more than 4 routes, a bound that some block reaches. `lengths`: of each device's 8 sequences one holds exactly 256 positions, the others at most 64. `page_table`: entries index the device's own pool of 44 pages; the first ceil(lengths / 16) entries of a row hold its positions in order and are distinct over all of the device's sequences; later entries are arbitrary.
All inputs are finite; a program needn't handle non-finite values.
Results may differ from the reference program's by a relative error of at most 0.0071.
Values may be sent and summed in bfloat16 or wider, within the bound.
A program may use at most 256 MiB of HBM per device.

```python
import math
import jax
import jax.numpy as jnp
import numpy as np
from jax import lax

D = 4096
FF = 1536
HEADS = 64
KV_HEADS = 4
HEAD_DIM = 128
TOP = 8
EXPERTS = 32
SEQ_DEV = 8
PAGE = 16
MAXP = 16
LMAX = 256
POOL = 44
MOST = 4
SPLIT = 1
HW = 1536
TOKENS = 128
PAGES_ALL = 704
N_SIDE = 2
N_DEV = 8


def kv_rows(key, count):
    first, second = jax.random.split(key)
    keys_part = jax.random.truncated_normal(first, -4.0, 4.0, (count, KV_HEADS, HEAD_DIM))
    values_part = jax.random.truncated_normal(second, -4.0, 4.0, (count, KV_HEADS, HEAD_DIM))
    return jnp.stack([keys_part, values_part], axis=1).reshape(count, 2 * KV_HEADS * HEAD_DIM)


def shuffle_pool(subkey):
    return jax.random.permutation(subkey, POOL).astype(jnp.int32)


def pick_pages(order, spots):
    return order[spots]


def paging(key):
    key = jax.random.fold_in(key, 101)
    first, second, third, fourth = jax.random.split(key, 4)
    blocks = TOKENS // SEQ_DEV
    long_pos = jax.random.randint(first, (blocks, 1), 0, SEQ_DEV)
    short = jax.random.randint(second, (blocks, SEQ_DEV), 1, LMAX // 4 + 1)
    slot_pos = jnp.arange(SEQ_DEV, dtype=jnp.int32)[None, :]
    lengths_all = jnp.where(slot_pos == long_pos, LMAX, short).astype(jnp.int32)
    used = (lengths_all + PAGE - 1) // PAGE
    begin = jnp.cumsum(used, axis=1) - used
    orders = jax.vmap(shuffle_pool)(jax.random.split(third, blocks))
    entry = jnp.arange(MAXP, dtype=jnp.int32)[None, None, :]
    spots = (begin[:, :, None] + entry) % POOL
    chosen = jax.vmap(pick_pages)(orders, spots)
    filler = jax.random.randint(fourth, (blocks, SEQ_DEV, MAXP), 0, POOL)
    table = jnp.where(entry < used[:, :, None], chosen, filler).astype(jnp.int32)
    return (lengths_all.reshape(TOKENS), table.reshape(TOKENS, MAXP))


def draw_lengths(key, part):
    return paging(key)[0]


def draw_page_table(key, part):
    return paging(key)[1]


def draw_queries(key, part):
    key = jax.random.fold_in(key, 3)
    second = jax.random.fold_in(key, 1)
    shape = (TOKENS, KV_HEADS, HEADS // KV_HEADS, HEAD_DIM)
    values = jax.random.truncated_normal(second, -4.0, 4.0, shape)
    return values.reshape(TOKENS, HEADS * HEAD_DIM).astype(jnp.bfloat16)


def draw_kv_cache(key, part):
    key = jax.random.fold_in(key, 5)
    values = kv_rows(key, PAGES_ALL * PAGE)
    return values.reshape(PAGES_ALL, PAGE, 2 * KV_HEADS * HEAD_DIM).astype(jnp.bfloat16)


def draw_new_kv(key, part):
    key = jax.random.fold_in(key, 7)
    values = kv_rows(key, TOKENS)
    return values.astype(jnp.bfloat16)


def block_scale(rng, extent, cuts, smallest, largest):
    gain = 1.0
    for dim, blocks in cuts:
        draws = jax.random.uniform(jax.random.fold_in(jax.random.fold_in(rng, 6), dim), (blocks,), jnp.float32, smallest / len(cuts), largest / len(cuts))
        gain = gain * jnp.repeat(jnp.exp(draws), extent[dim] // blocks).reshape((-1,) + (1,) * (len(extent) - 1 - dim))
    return gain


def shared_out(stream_key, own, number, rows, count, top, most, lean):
    sequence = jax.random.permutation(stream_key, count)
    crowded, common = load_shares(count, rows * top, most, lean, True), load_shares(count, rows * top, most, lean, False)
    places = jnp.arange(count)

    def named(sizes, turn):
        used = int((sizes > 0).sum())
        fixed = max(1, used // 4)
        moved = fixed + (places - fixed + turn * (used - fixed)) % max(1, count - fixed)
        return jnp.zeros((count,), jnp.int32).at[sequence[jnp.where(places < fixed, places, moved)]].set(jnp.asarray(sizes, jnp.int32))

    sizes = jnp.where(number % 4 == 0, named(crowded, number // 4), named(common, number - number // 4 - 1))
    mixed = jax.random.permutation(jax.random.fold_in(own, 3), count)
    giver, sink = mixed[0:count // 2 * 2:2], mixed[1:count // 2 * 2:2]
    slack = jnp.minimum(sizes[giver] - 1, most - sizes[sink]) // 2
    slack = jnp.where((giver == sequence[0]) | (sink == sequence[0]) | (sizes[sink] == 0), 0, jnp.maximum(slack, 0))
    moved = jax.random.randint(jax.random.fold_in(own, 4), (count // 2,), 0, 1 << 20) % (slack + 1)
    sizes = sizes.at[giver].add(-moved).at[sink].add(moved)
    members = jnp.searchsorted(jnp.cumsum(sizes), jnp.arange(rows * top), side="right").astype(jnp.int32)
    table = members.reshape(top, rows).T
    table = table[jax.random.permutation(jax.random.fold_in(own, 1), rows)]
    turn = jax.random.randint(jax.random.fold_in(own, 2), (rows, 1), 0, top)
    return jnp.take_along_axis(table, (jnp.arange(top)[None, :] + turn) % top, axis=1)


def load_shares(count, total, most, slope, full):
    portions = [(1 << 20) // math.isqrt(rank ** slope) + 1 for rank in range(1, count + 1)]
    largest = most if full else min(most, max(-(-total // count), total * portions[0] // sum(portions)))
    least = 1 if total - largest >= count - 1 else 0
    counts, spare = [largest] + [least] * (count - 1), total - largest - least * (count - 1)
    while spare > 0:
        free = [i for i in range(1, count) if counts[i] < largest] or [i for i in range(1, count) if counts[i] < most]
        whole, budget = sum([portions[i] for i in free]), spare
        for i in free:
            extra = min(most - counts[i], max(1, budget * portions[i] // whole), spare)
            counts[i] = counts[i] + extra
            spare = spare - extra
    return np.array(counts)


def bell_draw(key, extent, scale, limit, cuts=(), kind=jnp.bfloat16):
    level = block_scale(key, extent, cuts, -0.22, 0.18) if cuts else 1.0
    entries = jax.random.normal(key, extent, jnp.float32) * scale * level
    return jnp.minimum(jnp.maximum(entries, -limit), limit).astype(kind)


def setup_inputs(seed: int = 0, part: int = 0) -> dict:
    key_list = jax.random.split(jax.random.key(seed), 13)
    part_splits = jax.random.split(jax.random.fold_in(key_list[12], part), 13)
    queries = draw_queries(jax.random.fold_in(jax.random.fold_in(key_list[12], part), 71), part)
    kv_cache = draw_kv_cache(jax.random.fold_in(jax.random.fold_in(key_list[12], part), 71), part)
    new_kv = draw_new_kv(jax.random.fold_in(jax.random.fold_in(key_list[12], part), 71), part)
    lengths = draw_lengths(jax.random.fold_in(jax.random.fold_in(key_list[12], part), 71), part)
    page_table = draw_page_table(jax.random.fold_in(jax.random.fold_in(key_list[12], part), 71), part)
    hidden = bell_draw(part_splits[5], (TOKENS, D), 1.0, 6.0, ((0, 16),))
    norm_gain = jnp.clip(1.0 + 0.1 * jax.random.normal(key_list[6], (D,), jnp.float32), 0.5, 1.5)
    route_ids_keys = jax.random.split(jax.random.fold_in(part_splits[7], 1), TOKENS // SEQ_DEV)
    route_ids_turns = jax.random.permutation(jax.random.fold_in(part_splits[7], 3), TOKENS // SEQ_DEV)
    route_ids = jax.vmap(lambda own, number: shared_out(jax.random.fold_in(part_splits[7], 2), own, number, SEQ_DEV, EXPERTS, TOP, MOST, 2))(route_ids_keys, route_ids_turns).reshape((TOKENS, TOP))
    route_weights = jnp.clip(jnp.exp(math.log(1.0) - 2.9957323 * jax.random.uniform(part_splits[8], (TOKENS, TOP), jnp.float32) ** block_scale(part_splits[8], (TOKENS, TOP), ((0, 16),), -0.2, 0.2)), 0.05, 1.0)
    gate_w = bell_draw(key_list[9], (D, EXPERTS * FF), D ** -0.5, 0.09375, ((1, 16),))
    up_w = bell_draw(key_list[10], (D, EXPERTS * FF), D ** -0.5, 0.09375, ((1, 16),))
    down_w = bell_draw(key_list[11], (EXPERTS * FF, D), FF ** -0.5, 0.15625, ((0, 16),))
    return dict(queries=queries, kv_cache=kv_cache, new_kv=new_kv, lengths=lengths, page_table=page_table, hidden=hidden, norm_gain=norm_gain, route_ids=route_ids, route_weights=route_weights, gate_w=gate_w, up_w=up_w, down_w=down_w)


eps = 1e-06

def attend_block(queries, cache_pool, page_table, lengths, new_kv):
    seq_count = queries.shape[0]
    groups = HEADS // KV_HEADS
    paged = cache_pool[page_table].reshape(seq_count, MAXP * PAGE, 2, KV_HEADS, HEAD_DIM).astype(jnp.float32)
    cached_keys = paged[:, :, 0]
    cached_values = paged[:, :, 1]
    query_heads = queries.reshape(seq_count, KV_HEADS, groups, HEAD_DIM).astype(jnp.float32)
    fresh = new_kv.reshape(seq_count, 2, KV_HEADS, HEAD_DIM).astype(jnp.float32)
    factor = HEAD_DIM ** (-0.5)
    scores = jnp.einsum('rkgd,rlkd->rkgl', query_heads, cached_keys) * factor
    self_score = jnp.einsum('rkgd,rkd->rkg', query_heads, fresh[:, 0]) * factor
    valid = (jnp.arange(MAXP * PAGE, dtype=jnp.int32)[None, :] < lengths[:, None])[:, None, None, :]
    highest = jnp.maximum(lax.optimization_barrier(jnp.max(jnp.where(valid, scores, -1e+30), axis=-1)), self_score)
    expo = jnp.where(valid, jnp.exp(scores - highest[..., None]), 0.0)
    self_expo = jnp.exp(self_score - highest)
    denom = lax.optimization_barrier(jnp.sum(expo, axis=-1)) + self_expo
    probs = lax.optimization_barrier(expo.astype(jnp.bfloat16)).astype(jnp.float32)
    self_prob = lax.optimization_barrier(self_expo.astype(jnp.bfloat16)).astype(jnp.float32)
    mixed = jnp.einsum('rkgl,rlkd->rkgd', probs, cached_values)
    mixed = mixed + self_prob[..., None] * fresh[:, 1][:, :, None, :]
    return (mixed / denom[..., None]).astype(jnp.bfloat16).reshape(seq_count, HEADS * HEAD_DIM)

def route_slots(expert_ids):
    flat_ids = expert_ids.reshape(-1)
    onehot = (flat_ids[:, None] == jnp.arange(EXPERTS, dtype=jnp.int32)[None, :]).astype(jnp.int32)
    earlier = jnp.cumsum(onehot, axis=0) - onehot
    return (flat_ids, lax.optimization_barrier(jnp.sum(earlier * onehot, axis=1)).astype(jnp.int32))

def reference(queries, kv_cache, new_kv, lengths, page_table, hidden, norm_gain, route_ids, route_weights, gate_w, up_w, down_w):
    devices = N_SIDE * N_DEV
    width_kv = 2 * KV_HEADS * HEAD_DIM

    def one_block(packed):
        return attend_block(packed[0], packed[1], packed[2], packed[3], packed[4])
    context = lax.map(one_block, (queries.reshape(devices, SEQ_DEV, HEADS * HEAD_DIM), kv_cache.reshape(devices, POOL, PAGE, width_kv), page_table.reshape(devices, SEQ_DEV, MAXP), lengths.reshape(devices, SEQ_DEV), new_kv.reshape(devices, SEQ_DEV, width_kv)))
    context = context.reshape(TOKENS, HEADS * HEAD_DIM)
    wide = hidden.astype(jnp.float32)
    normed = (wide * lax.rsqrt(lax.optimization_barrier(jnp.mean(wide * wide, axis=-1, keepdims=True)) + eps) * norm_gain).astype(jnp.bfloat16)
    weights = route_weights / lax.optimization_barrier(jnp.sum(route_weights, axis=-1, keepdims=True))
    block_ids, block_ranks = jax.vmap(route_slots)(route_ids.reshape(devices, SEQ_DEV * TOP))
    source = jnp.arange(devices, dtype=jnp.int32)[:, None]
    position = jnp.arange(SEQ_DEV * TOP, dtype=jnp.int32)[None, :]
    token_index = (source * SEQ_DEV + position // TOP).astype(jnp.int32)
    column = (source * MOST + block_ranks).astype(jnp.int32)
    slot_token = jnp.full((EXPERTS, devices * MOST), TOKENS, jnp.int32).at[block_ids, column].set(token_index)
    slot_weight = jnp.zeros((EXPERTS, devices * MOST), jnp.float32).at[block_ids, column].set(weights.reshape(devices, SEQ_DEV * TOP))

    def expert_step(carry, expert):
        chosen = jnp.take(normed, slot_token[expert], axis=0, mode='fill', fill_value=0)
        result = jnp.zeros((devices * MOST, D), jnp.float32)
        for portion in range(SPLIT):
            start = (expert * FF + portion * HW).astype(jnp.int32)
            gate_part = lax.dynamic_slice_in_dim(gate_w, start, HW, 1)
            up_part = lax.dynamic_slice_in_dim(up_w, start, HW, 1)
            down_part = lax.dynamic_slice_in_dim(down_w, start, HW, 0)
            gate_val = jnp.dot(chosen, gate_part, preferred_element_type=jnp.float32)
            up_val = jnp.dot(chosen, up_part, preferred_element_type=jnp.float32)
            activation = (jax.nn.silu(gate_val) * up_val).astype(jnp.bfloat16)
            partial_value = jnp.dot(activation, down_part, preferred_element_type=jnp.float32).astype(jnp.bfloat16)
            result = result + lax.optimization_barrier(partial_value).astype(jnp.float32)
        carry = carry.at[slot_token[expert]].add(slot_weight[expert][:, None] * result, mode='drop')
        return (carry, expert)
    moe_sum = lax.scan(expert_step, jnp.zeros((TOKENS, D), jnp.float32), jnp.arange(EXPERTS, dtype=jnp.int32))[0]
    return (context, moe_sum.astype(jnp.bfloat16))
```

```python
import functools

import jax
import jax.numpy as jnp
from jax import lax
from jax.experimental import pallas as pl
from jax.experimental.pallas import tpu as pltpu
from jax.sharding import PartitionSpec as P

FF = 1536
HEADS = 64
KV_HEADS = 4
HEAD_DIM = 128
EXPERTS = 32
PAGE = 16
MAXP = 16
GROUP = HEADS // KV_HEADS
AXES = ("side", "dev")
eps = 1e-06


def attend(q_ref, kv_ref, new_ref, len_ref, table_ref, out_ref):
    seqs = q_ref.shape[0]
    positions = kv_ref.shape[0]
    where = lax.broadcasted_iota(jnp.int32, (seqs, positions), 1)
    page, offset = where >> 4, where & 15
    lengths = len_ref[...]
    table = table_ref[...]
    valid = jnp.zeros((seqs, positions), jnp.int32)
    for j in range(MAXP):
        hit = (table[:, j : j + 1] == page) & (offset + j * PAGE < lengths)
        valid = valid | hit.astype(jnp.int32)
    bias = jnp.where(valid > 0, 0.0, -1e30)[:, None, :]
    valid3 = jnp.broadcast_to(bias, (seqs, GROUP, positions)) == 0.0
    factor = HEAD_DIM ** (-0.5)
    for g in range(KV_HEADS):
        cols = slice(g * HEAD_DIM, (g + 1) * HEAD_DIM)
        vcols = slice((KV_HEADS + g) * HEAD_DIM, (KV_HEADS + g + 1) * HEAD_DIM)
        q3 = q_ref[:, g * GROUP : (g + 1) * GROUP, :]
        scores = lax.dot_general(
            q3.reshape(seqs * GROUP, HEAD_DIM),
            kv_ref[:, cols],
            (((1,), (1,)), ((), ())),
            preferred_element_type=jnp.float32,
        ).reshape(seqs, GROUP, positions)
        scores = jnp.where(valid3, scores * factor, -1e30)
        own = new_ref[:, cols].astype(jnp.float32)[:, None, :]
        self_score = jnp.sum(q3.astype(jnp.float32) * own, axis=-1, keepdims=True) * factor
        highest = jnp.maximum(jnp.max(scores, axis=-1, keepdims=True), self_score)
        expo = jnp.exp(scores - highest)
        self_expo = jnp.exp(self_score - highest)
        denom = jnp.sum(expo, axis=-1, keepdims=True) + self_expo
        mixed = jnp.dot(
            expo.astype(jnp.bfloat16).reshape(seqs * GROUP, positions),
            kv_ref[:, vcols],
            preferred_element_type=jnp.float32,
        ).reshape(seqs, GROUP, HEAD_DIM)
        fresh = new_ref[:, vcols].astype(jnp.float32)[:, None, :]
        total = mixed + self_expo.astype(jnp.bfloat16).astype(jnp.float32) * fresh
        out_ref[:, g * GROUP : (g + 1) * GROUP, :] = (total / denom).astype(jnp.bfloat16)


def experts(x_ref, g_ref, gate_ref, up_ref, down_ref, out_ref, total):
    step = pl.program_id(0)

    @pl.when(step == 0)
    def _():
        total[...] = jnp.zeros_like(total)

    x = x_ref[...]
    gate = jnp.dot(x, gate_ref[...], preferred_element_type=jnp.float32)
    up = jnp.dot(x, up_ref[...], preferred_element_type=jnp.float32)
    act = (gate / (1.0 + jnp.exp(-gate)) * up).astype(jnp.bfloat16)
    total[...] += g_ref[0] * jnp.dot(act, down_ref[...], preferred_element_type=jnp.float32)

    @pl.when(step == pl.num_programs(0) - 1)
    def _():
        out_ref[...] = total[...].astype(jnp.bfloat16)


def on_device(
    queries,
    kv_cache,
    new_kv,
    lengths,
    page_table,
    hidden,
    norm_gain,
    route_ids,
    route_weights,
    gate_w,
    up_w,
    down_w,
):
    seqs, depth = hidden.shape
    wide = hidden.astype(jnp.float32)
    normed = (
        wide * lax.rsqrt(jnp.mean(wide * wide, axis=-1, keepdims=True) + eps) * norm_gain
    ).astype(jnp.bfloat16)
    weights = route_weights / jnp.sum(route_weights, axis=-1, keepdims=True)
    dense = jnp.sum(
        jnp.where(
            route_ids[:, :, None] == jnp.arange(EXPERTS, dtype=jnp.int32), weights[:, :, None], 0.0
        ),
        axis=1,
    )
    tokens = lax.all_gather(normed, AXES, axis=0, tiled=True)
    gates = lax.all_gather(dense, AXES, axis=0, tiled=True)

    positions = kv_cache.shape[0] * PAGE
    context = pl.pallas_call(
        attend,
        out_shape=jax.ShapeDtypeStruct((seqs, HEADS, HEAD_DIM), jnp.bfloat16),
        compiler_params=pltpu.CompilerParams(vmem_limit_bytes=32 << 20),
        cost_estimate=pl.CostEstimate(flops=400_000_000, bytes_accessed=2_000_000, transcendentals=400_000),
    )(
        queries.reshape(seqs, HEADS, HEAD_DIM),
        kv_cache.reshape(positions, -1),
        new_kv,
        lengths.reshape(seqs, 1),
        page_table,
    ).reshape(seqs, HEADS * HEAD_DIM)

    columns = gate_w.shape[1]
    units = min(columns, FF)
    per_device = max(columns // FF, 1)
    device = lax.axis_index(AXES)
    count = tokens.shape[0]
    mine = lax.dynamic_slice(gates, (0, device * columns // FF), (count, per_device))
    mine = mine.T.reshape(per_device, count, 1)
    tile = 256 if units % 256 == 0 else 128
    per_expert = units // tile
    part = pl.pallas_call(
        experts,
        out_shape=jax.ShapeDtypeStruct((count, depth), jnp.bfloat16),
        grid=(columns // tile,),
        in_specs=[
            pl.BlockSpec((count, depth), lambda i: (0, 0)),
            pl.BlockSpec((1, count, 1), lambda i: (i // per_expert, 0, 0)),
            pl.BlockSpec((depth, tile), lambda i: (0, i)),
            pl.BlockSpec((depth, tile), lambda i: (0, i)),
            pl.BlockSpec((tile, depth), lambda i: (i, 0)),
        ],
        out_specs=pl.BlockSpec((count, depth), lambda i: (0, 0)),
        scratch_shapes=[pltpu.VMEM((count, depth), jnp.float32)],
        compiler_params=pltpu.CompilerParams(vmem_limit_bytes=60 << 20),
    )(tokens, mine, gate_w, up_w, down_w)

    devices = lax.axis_size(AXES)
    back = lax.all_to_all(
        part.reshape(devices, seqs, depth), AXES, split_axis=0, concat_axis=0, tiled=True
    )
    moe_out = jnp.sum(back.astype(jnp.float32), axis=0).astype(jnp.bfloat16)
    return (context, moe_out)


def solution(mesh):
    rows = P(("groups", "side", "dev"), None)
    placed = (
        rows,
        P(("groups", "side", "dev"), None, None),
        rows,
        P(("groups", "side", "dev")),
        rows,
        rows,
        P(),
        rows,
        rows,
        P(None, ("side", "dev")),
        P(None, ("side", "dev")),
        P(("side", "dev"), None),
    )
    return jax.shard_map(
        on_device, mesh=mesh, in_specs=placed, out_specs=(rows, rows), check_vma=False
    )
```

```python
import functools

import jax
import jax.numpy as jnp
from jax import lax
from jax.experimental import pallas as pl
from jax.experimental.pallas import tpu as pltpu
from jax.sharding import PartitionSpec as P

FF = 1536
HEADS = 64
KV_HEADS = 4
HEAD_DIM = 128
EXPERTS = 32
PAGE = 16
MAXP = 16
GROUP = HEADS // KV_HEADS
eps = 1e-06


def attend(q_ref, kv_ref, new_ref, len_ref, table_ref, out_ref):
    seqs = q_ref.shape[0]
    positions = kv_ref.shape[0]
    where = lax.broadcasted_iota(jnp.int32, (seqs, positions), 1)
    page, offset = where >> 4, where & 15
    lengths = len_ref[...]
    table = table_ref[...]
    valid = jnp.zeros((seqs, positions), jnp.int32)
    for j in range(MAXP):
        hit = (table[:, j : j + 1] == page) & (offset + j * PAGE < lengths)
        valid = valid | hit.astype(jnp.int32)
    bias = jnp.where(valid > 0, 0.0, -1e30)[:, None, :]
    valid3 = jnp.broadcast_to(bias, (seqs, GROUP, positions)) == 0.0
    factor = HEAD_DIM ** (-0.5)
    for g in range(KV_HEADS):
        cols = slice(g * HEAD_DIM, (g + 1) * HEAD_DIM)
        vcols = slice((KV_HEADS + g) * HEAD_DIM, (KV_HEADS + g + 1) * HEAD_DIM)
        q3 = q_ref[:, g * GROUP : (g + 1) * GROUP, :]
        scores = lax.dot_general(
            q3.reshape(seqs * GROUP, HEAD_DIM),
            kv_ref[:, cols],
            (((1,), (1,)), ((), ())),
            preferred_element_type=jnp.float32,
        ).reshape(seqs, GROUP, positions)
        scores = jnp.where(valid3, scores * factor, -1e30)
        own = new_ref[:, cols].astype(jnp.float32)[:, None, :]
        self_score = jnp.sum(q3.astype(jnp.float32) * own, axis=-1, keepdims=True) * factor
        highest = jnp.maximum(jnp.max(scores, axis=-1, keepdims=True), self_score)
        expo = jnp.exp(scores - highest)
        self_expo = jnp.exp(self_score - highest)
        denom = jnp.sum(expo, axis=-1, keepdims=True) + self_expo
        mixed = jnp.dot(
            expo.astype(jnp.bfloat16).reshape(seqs * GROUP, positions),
            kv_ref[:, vcols],
            preferred_element_type=jnp.float32,
        ).reshape(seqs, GROUP, HEAD_DIM)
        fresh = new_ref[:, vcols].astype(jnp.float32)[:, None, :]
        total = mixed + self_expo.astype(jnp.bfloat16).astype(jnp.float32) * fresh
        out_ref[:, g * GROUP : (g + 1) * GROUP, :] = (total / denom).astype(jnp.bfloat16)


def layer(
    n,
    tile,
    block,
    q_ref,
    kv_ref,
    new_ref,
    len_ref,
    table_ref,
    hid_ref,
    gain_ref,
    ids_ref,
    rw_ref,
    gate_hbm,
    up_hbm,
    down_hbm,
    ctx_ref,
    moe_ref,
    gate_buf,
    up_buf,
    down_buf,
    packed,
    x_buf,
    g_buf,
    act_buf,
    y_buf,
    half_out,
    half_in,
    z_out,
    z_in,
    gate_sem,
    up_sem,
    down_sem,
    tok_sem,
    half_sem,
    z_sem,
):
    side, me = lax.axis_index("side"), lax.axis_index("dev")
    seqs, depth = hid_ref.shape
    half = depth // 2
    columns = gate_hbm.shape[1]
    steps, slots = columns // tile, gate_buf.shape[0]
    blocks, down_slots = depth // block, down_buf.shape[0]
    per_expert = min(columns, FF) // tile
    first = (side * n + me) * columns // FF

    def fetch(i):
        slot = lax.rem(i, slots)
        cols = pl.ds(pl.multiple_of(i * tile, tile), tile)
        return (
            pltpu.make_async_copy(gate_hbm.at[:, cols], gate_buf.at[slot], gate_sem.at[slot]),
            pltpu.make_async_copy(up_hbm.at[:, cols], up_buf.at[slot], up_sem.at[slot]),
        )

    def fetch_down(c):
        slot = lax.rem(c, down_slots)
        cols = pl.ds(pl.multiple_of(c * block, block), block)
        return pltpu.make_async_copy(down_hbm.at[:, cols], down_buf.at[slot], down_sem.at[slot])

    @pl.loop(0, slots)
    def _(i):
        for copy in fetch(i):
            copy.start()

    @pl.loop(0, down_slots)
    def _(c):
        fetch_down(c).start()

    barrier = pltpu.get_barrier_semaphore()
    pl.semaphore_signal(
        barrier, inc=1, device_id={"side": 1 - side}, device_id_type=pl.DeviceIdType.MESH
    )

    @pl.loop(1, n)
    def _(k):
        pl.semaphore_signal(
            barrier,
            inc=1,
            device_id={"dev": lax.rem(me + k, n)},
            device_id_type=pl.DeviceIdType.MESH,
        )

    wide = hid_ref[...].astype(jnp.float32)
    scale = lax.rsqrt(jnp.mean(wide * wide, axis=-1, keepdims=True) + eps)
    normed = wide * scale * gain_ref[...]
    rw = rw_ref[...]
    rw = rw / jnp.sum(rw, axis=-1, keepdims=True)
    ids = ids_ref[...]
    lane = lax.broadcasted_iota(jnp.int32, (seqs, 128), 1)
    dense = jnp.zeros((seqs, 128), jnp.float32)
    for j in range(ids.shape[1]):
        dense = dense + jnp.where(ids[:, j : j + 1] == (lane & 31), rw[:, j : j + 1], 0.0)
    top = dense.astype(jnp.bfloat16).astype(jnp.float32)
    rest = dense - top
    middle = rest.astype(jnp.bfloat16).astype(jnp.float32)
    terms = jnp.where(lane < 32, top, jnp.where(lane < 64, middle, rest - middle))
    terms = jnp.where(lane < 96, terms, 0.0)
    mine = side * n + me
    packed[mine, :, :half] = jnp.concatenate([normed[:, :half], normed[:, half:]], axis=0).astype(
        jnp.bfloat16
    )
    packed[mine, :, half:] = jnp.concatenate([terms, terms], axis=0).astype(jnp.bfloat16)

    pl.semaphore_wait(barrier, n)

    @pl.loop(1, n)
    def _(k):
        pltpu.make_async_remote_copy(
            src_ref=packed.at[mine],
            dst_ref=packed.at[mine],
            send_sem=tok_sem.at[0],
            recv_sem=tok_sem.at[1],
            device_id={"dev": lax.rem(me + k, n)},
            device_id_type=pl.DeviceIdType.MESH,
        ).start()

    attend(q_ref, kv_ref, new_ref, len_ref, table_ref, ctx_ref)

    others = packed.at[pl.ds(0, n - 1)]
    pltpu.make_async_copy(others, others, tok_sem.at[1]).wait()
    own_side = packed.at[pl.ds(side * n, n)]
    swap = pltpu.make_async_remote_copy(
        src_ref=own_side,
        dst_ref=own_side,
        send_sem=tok_sem.at[2],
        recv_sem=tok_sem.at[3],
        device_id={"side": 1 - side},
        device_id_type=pl.DeviceIdType.MESH,
    )
    swap.start()
    swap.wait()
    pltpu.make_async_copy(others, others, tok_sem.at[0]).wait()

    @pl.loop(0, n)
    def _(p):
        both = packed[pl.ds(2 * p, 2)].astype(jnp.float32)
        rows = pl.ds(pl.multiple_of(p * 2 * seqs, 2 * seqs), 2 * seqs)
        low = both[:, :seqs, :half].reshape(2 * seqs, half)
        high = both[:, seqs:, :half].reshape(2 * seqs, half)
        x_buf[rows, :half] = low.astype(jnp.bfloat16)
        x_buf[rows, half:] = high.astype(jnp.bfloat16)
        g_buf[rows, :] = both[:, :seqs, half:].reshape(2 * seqs, 128)

    @pl.loop(0, steps)
    def _(i):
        slot = lax.rem(i, slots)
        for copy in fetch(i):
            copy.wait()
        x = x_buf[...]
        gate = jnp.dot(x, gate_buf[slot], preferred_element_type=jnp.float32)
        up = jnp.dot(x, up_buf[slot], preferred_element_type=jnp.float32)
        terms = g_buf[...]
        place = lax.broadcasted_iota(jnp.int32, terms.shape, 1) & 31
        share = jnp.sum(
            jnp.where(place == first + i // per_expert, terms, 0.0), axis=1, keepdims=True
        )
        act = gate / (1.0 + jnp.exp(-gate)) * up * share
        act_buf[:, pl.ds(pl.multiple_of(i * tile, tile), tile)] = act.astype(jnp.bfloat16)

        @pl.when(i + slots < steps)
        def _():
            for copy in fetch(i + slots):
                copy.start()

    def to_partner(c):
        return pltpu.make_async_remote_copy(
            src_ref=half_out.at[c],
            dst_ref=half_in.at[c],
            send_sem=half_sem.at[0, c],
            recv_sem=half_sem.at[1, c],
            device_id={"side": 1 - side},
            device_id_type=pl.DeviceIdType.MESH,
        )

    def multiply(c):
        slot = lax.rem(c, down_slots)
        fetch_down(c).wait()
        y = jnp.dot(act_buf[...], down_buf[slot], preferred_element_type=jnp.float32)
        y_buf[lax.rem(c, 2)] = y.reshape(2, n * seqs, block)
        half_out[c] = y_buf[lax.rem(c, 2), 1 - side].astype(jnp.bfloat16)
        to_partner(c).start()

        @pl.when(c + down_slots < blocks)
        def _():
            fetch_down(c + down_slots).start()

    def spread(c):
        to_partner(c).wait_recv()
        total = y_buf[lax.rem(c, 2), side] + half_in[c].astype(jnp.float32)
        total = total.reshape(n, seqs, block)
        z_out[c] = jnp.concatenate(
            [total[:, :, : block // 2], total[:, :, block // 2 :]], axis=1
        ).astype(jnp.bfloat16)

        @pl.loop(1, n)
        def _(k):
            to = lax.rem(me + k, n)
            pltpu.make_async_remote_copy(
                src_ref=z_out.at[c, to],
                dst_ref=z_in.at[c, k - 1],
                send_sem=z_sem.at[0, c],
                recv_sem=z_sem.at[1, c],
                device_id={"dev": to},
                device_id_type=pl.DeviceIdType.MESH,
            ).start()

    multiply(0)

    @pl.loop(1, blocks)
    def _(c):
        multiply(c)
        spread(c - 1)

    spread(blocks - 1)

    @pl.loop(0, blocks)
    def _(c):
        pltpu.make_async_copy(z_in.at[c], z_in.at[c], z_sem.at[1, c]).wait()
        total = jnp.sum(z_in[c].astype(jnp.float32), axis=0) + z_out[c, me].astype(jnp.float32)
        merged = jnp.concatenate([total[:seqs], total[seqs:]], axis=1)
        moe_ref[:, pl.ds(pl.multiple_of(c * block, block), block)] = merged.astype(jnp.bfloat16)
        to_partner(c).wait_send()
        pltpu.make_async_copy(z_in.at[c], z_in.at[c], z_sem.at[0, c]).wait()


def on_device(
    queries,
    kv_cache,
    new_kv,
    lengths,
    page_table,
    hidden,
    norm_gain,
    route_ids,
    route_weights,
    gate_w,
    up_w,
    down_w,
):
    seqs, depth = hidden.shape
    positions = kv_cache.shape[0] * PAGE
    columns = gate_w.shape[1]
    units = min(columns, FF)
    n = lax.axis_size("dev")
    tokens = 2 * n * seqs
    tile = 256 if units % 256 == 0 else 128
    slots = min(columns // tile, 8)
    block = 512
    blocks = depth // block
    down_slots = min(blocks, 4)
    bf16 = jnp.bfloat16
    dma = pltpu.SemaphoreType.DMA
    vmem = pl.BlockSpec(memory_space=pltpu.VMEM)
    hbm = pl.BlockSpec(memory_space=pl.ANY)
    context, moe_out = pl.pallas_call(
        functools.partial(layer, n, tile, block),
        out_shape=(
            jax.ShapeDtypeStruct((seqs, HEADS, HEAD_DIM), bf16),
            jax.ShapeDtypeStruct((seqs, depth), bf16),
        ),
        in_specs=[vmem] * 9 + [hbm] * 3,
        out_specs=(vmem, vmem),
        scratch_shapes=[
            pltpu.VMEM((slots, depth, tile), bf16),
            pltpu.VMEM((slots, depth, tile), bf16),
            pltpu.VMEM((down_slots, columns, block), bf16),
            pltpu.VMEM((2 * n, 2 * seqs, depth // 2 + 128), bf16),
            pltpu.VMEM((tokens, depth), bf16),
            pltpu.VMEM((tokens, 128), jnp.float32),
            pltpu.VMEM((tokens, columns), bf16),
            pltpu.VMEM((2, 2, n * seqs, block), jnp.float32),
            pltpu.VMEM((blocks, n * seqs, block), bf16),
            pltpu.VMEM((blocks, n * seqs, block), bf16),
            pltpu.VMEM((blocks, n, 2 * seqs, block // 2), bf16),
            pltpu.VMEM((blocks, n - 1, 2 * seqs, block // 2), bf16),
            dma((slots,)),
            dma((slots,)),
            dma((down_slots,)),
            dma((4,)),
            dma((2, blocks)),
            dma((2, blocks)),
        ],
        compiler_params=pltpu.CompilerParams(
            collective_id=0, has_side_effects=True, vmem_limit_bytes=60 << 20
        ),
        cost_estimate=pl.CostEstimate(
            flops=6 * tokens * depth * columns,
            bytes_accessed=6 * depth * columns,
            transcendentals=tokens * columns,
        ),
    )(
        queries.reshape(seqs, HEADS, HEAD_DIM),
        kv_cache.reshape(positions, -1),
        new_kv,
        lengths.reshape(seqs, 1),
        page_table,
        hidden,
        norm_gain.reshape(1, depth),
        route_ids,
        route_weights,
        gate_w,
        up_w,
        down_w,
    )
    return (context.reshape(seqs, HEADS * HEAD_DIM), moe_out)


def solution(mesh):
    rows = P(("groups", "side", "dev"), None)
    placed = (
        rows,
        P(("groups", "side", "dev"), None, None),
        rows,
        P(("groups", "side", "dev")),
        rows,
        rows,
        P(),
        rows,
        rows,
        P(None, ("side", "dev")),
        P(None, ("side", "dev")),
        P(("side", "dev"), None),
    )
    return jax.shard_map(
        on_device, mesh=mesh, in_specs=placed, out_specs=(rows, rows), check_vma=False
    )
```

```python
import functools

import jax
import jax.numpy as jnp
from jax import lax
from jax.experimental import pallas as pl
from jax.experimental.pallas import tpu as pltpu
from jax.sharding import PartitionSpec as P

FF = 1536
HEADS = 64
KV_HEADS = 4
HEAD_DIM = 128
EXPERTS = 32
PAGE = 16
MAXP = 16
GROUP = HEADS // KV_HEADS
eps = 1e-06


def attend(q_ref, kv_ref, new_ref, len_ref, table_ref, out_ref):
    seqs = q_ref.shape[0]
    positions = kv_ref.shape[0]
    where = lax.broadcasted_iota(jnp.int32, (seqs, positions), 1)
    row = lax.broadcasted_iota(jnp.int32, (seqs, positions), 0)
    page, offset = where >> 4, where & 15
    lengths = jnp.zeros((seqs, positions), jnp.int32)
    for t in range(seqs):
        lengths = jnp.where(row == t, len_ref[t], lengths)
    table = table_ref[...]
    valid = jnp.zeros((seqs, positions), jnp.int32)
    for j in range(MAXP):
        hit = (table[:, j : j + 1] == page) & (offset + j * PAGE < lengths)
        valid = valid | hit.astype(jnp.int32)
    valid3 = jnp.broadcast_to(valid[None], (GROUP, seqs, positions)) > 0
    factor = HEAD_DIM ** (-0.5)
    for g in range(KV_HEADS):
        cols = slice(g * HEAD_DIM, (g + 1) * HEAD_DIM)
        vcols = slice((KV_HEADS + g) * HEAD_DIM, (KV_HEADS + g + 1) * HEAD_DIM)
        heads = [
            q_ref[:, h * HEAD_DIM : (h + 1) * HEAD_DIM].astype(jnp.float32)
            for h in range(g * GROUP, (g + 1) * GROUP)
        ]
        q = jnp.concatenate(heads, axis=0)
        scores = lax.dot_general(
            q.astype(jnp.bfloat16),
            kv_ref[:, cols],
            (((1,), (1,)), ((), ())),
            preferred_element_type=jnp.float32,
        ).reshape(GROUP, seqs, positions)
        scores = jnp.where(valid3, scores * factor, -1e30)
        own = new_ref[:, cols].astype(jnp.float32)[None]
        q3 = q.reshape(GROUP, seqs, HEAD_DIM)
        self_score = jnp.sum(q3 * own, axis=-1, keepdims=True) * factor
        highest = jnp.maximum(jnp.max(scores, axis=-1, keepdims=True), self_score)
        expo = jnp.exp(scores - highest)
        self_expo = jnp.exp(self_score - highest)
        denom = jnp.sum(expo, axis=-1, keepdims=True) + self_expo
        mixed = jnp.dot(
            expo.reshape(GROUP * seqs, positions).astype(jnp.bfloat16),
            kv_ref[:, vcols],
            preferred_element_type=jnp.float32,
        ).reshape(GROUP, seqs, HEAD_DIM)
        fresh = new_ref[:, vcols].astype(jnp.float32)[None]
        total = mixed + self_expo.astype(jnp.bfloat16).astype(jnp.float32) * fresh
        total = (total / denom).astype(jnp.bfloat16)
        for h in range(GROUP):
            at = (g * GROUP + h) * HEAD_DIM
            out_ref[:, at : at + HEAD_DIM] = total[h]


def layer(
    n,
    tile,
    block,
    q_ref,
    kv_ref,
    new_ref,
    len_ref,
    table_ref,
    hid_ref,
    gain_ref,
    ids_ref,
    rw_ref,
    gate_hbm,
    up_hbm,
    down_hbm,
    ctx_ref,
    moe_ref,
    gate_buf,
    up_buf,
    down_buf,
    packed,
    x_buf,
    g_buf,
    act_buf,
    y_buf,
    half_out,
    half_in,
    z_out,
    z_in,
    gate_sem,
    up_sem,
    down_sem,
    tok_sem,
    ring_sem,
    half_sem,
    z_sem,
):
    side, me = lax.axis_index("side"), lax.axis_index("dev")
    ranks = n // 2
    rank, odd = me // 2, me % 2
    mesh_id = pl.DeviceIdType.MESH
    partner, pair = {"side": 1 - side}, {"dev": rank * 2 + 1 - odd}
    seqs, depth = hid_ref.shape
    half = depth // 2
    columns = gate_hbm.shape[1]
    steps, slots = columns // tile, gate_buf.shape[0]
    blocks, down_slots = depth // block, down_buf.shape[0]
    per_expert = min(columns, FF) // tile
    first = (side * n + me) * columns // FF

    def fetch(i):
        slot = lax.rem(i, slots)
        cols = pl.ds(pl.multiple_of(i * tile, tile), tile)
        return (
            pltpu.make_async_copy(gate_hbm.at[:, cols], gate_buf.at[slot], gate_sem.at[slot]),
            pltpu.make_async_copy(up_hbm.at[:, cols], up_buf.at[slot], up_sem.at[slot]),
        )

    def fetch_down(c):
        slot = lax.rem(c, down_slots)
        cols = pl.ds(pl.multiple_of(c * block, block), block)
        return pltpu.make_async_copy(down_hbm.at[:, cols], down_buf.at[slot], down_sem.at[slot])

    @pl.loop(0, slots)
    def _(i):
        for copy in fetch(i):
            copy.start()

    @pl.loop(0, down_slots)
    def _(c):
        fetch_down(c).start()

    barrier = pltpu.get_barrier_semaphore()
    pl.semaphore_signal(
        barrier, inc=1, device_id=partner, device_id_type=mesh_id
    )

    @pl.loop(1, n)
    def _(k):
        pl.semaphore_signal(
            barrier,
            inc=1,
            device_id={"dev": lax.rem(me + k, n)},
            device_id_type=mesh_id,
        )

    def peer(k):
        return {"dev": lax.rem(rank + k, ranks) * 2 + odd}

    wide = hid_ref[...].astype(jnp.float32)
    scale = lax.rsqrt(jnp.mean(wide * wide, axis=-1, keepdims=True) + eps)
    normed = wide * scale * gain_ref[...]
    rw = rw_ref[...]
    rw = rw / jnp.sum(rw, axis=-1, keepdims=True)
    ids = ids_ref[...]
    lane = lax.broadcasted_iota(jnp.int32, (seqs, 128), 1)
    dense = jnp.zeros((seqs, 128), jnp.float32)
    for j in range(ids.shape[1]):
        dense = dense + jnp.where(ids[:, j : j + 1] == (lane & 31), rw[:, j : j + 1], 0.0)
    top = dense.astype(jnp.bfloat16).astype(jnp.float32)
    rest = dense - top
    middle = rest.astype(jnp.bfloat16).astype(jnp.float32)
    terms = jnp.where(lane < 32, top, jnp.where(lane < 64, middle, rest - middle))
    terms = jnp.where(lane < 96, terms, 0.0)
    mine = side * n + me
    packed[mine, :, :half] = jnp.concatenate([normed[:, :half], normed[:, half:]], axis=0).astype(
        jnp.bfloat16
    )
    packed[mine, :, half:] = jnp.concatenate([terms, terms], axis=0).astype(jnp.bfloat16)

    pl.semaphore_wait(barrier, n)

    @pl.loop(1, ranks)
    def _(k):
        pltpu.make_async_remote_copy(
            src_ref=packed.at[mine],
            dst_ref=packed.at[mine],
            send_sem=tok_sem.at[0],
            recv_sem=ring_sem.at[k],
            device_id=peer(k),
            device_id_type=mesh_id,
        ).start()

    def forward(index):
        pltpu.make_async_remote_copy(
            src_ref=packed.at[index],
            dst_ref=packed.at[index],
            send_sem=tok_sem.at[1],
            recv_sem=tok_sem.at[4],
            device_id=pair,
            device_id_type=mesh_id,
        ).start()

    forward(mine)
    attend(q_ref, kv_ref, new_ref, len_ref, table_ref, ctx_ref)

    @pl.loop(1, ranks)
    def _(k):
        index = side * n + lax.rem(rank - k + ranks, ranks) * 2 + odd
        pltpu.make_async_copy(packed.at[index], packed.at[index], ring_sem.at[k]).wait()
        forward(index)

    others = packed.at[pl.ds(0, ranks - 1)]
    whole = packed.at[pl.ds(0, ranks)]
    pltpu.make_async_copy(whole, whole, tok_sem.at[4]).wait()
    own_side = packed.at[pl.ds(side * n, n)]
    swap = pltpu.make_async_remote_copy(
        src_ref=own_side,
        dst_ref=own_side,
        send_sem=tok_sem.at[2],
        recv_sem=tok_sem.at[3],
        device_id=partner,
        device_id_type=mesh_id,
    )
    swap.start()
    swap.wait()
    pltpu.make_async_copy(others, others, tok_sem.at[0]).wait()
    pltpu.make_async_copy(whole, whole, tok_sem.at[1]).wait()

    @pl.loop(0, n)
    def _(p):
        both = packed[pl.ds(2 * p, 2)].astype(jnp.float32)
        rows = pl.ds(pl.multiple_of(p * 2 * seqs, 2 * seqs), 2 * seqs)
        low = both[:, :seqs, :half].reshape(2 * seqs, half)
        high = both[:, seqs:, :half].reshape(2 * seqs, half)
        x_buf[rows, :half] = low.astype(jnp.bfloat16)
        x_buf[rows, half:] = high.astype(jnp.bfloat16)
        g_buf[rows, :] = both[:, :seqs, half:].reshape(2 * seqs, 128)

    @pl.loop(0, steps)
    def _(i):
        slot = lax.rem(i, slots)
        for copy in fetch(i):
            copy.wait()
        x = x_buf[...]
        gate = jnp.dot(x, gate_buf[slot], preferred_element_type=jnp.float32)
        up = jnp.dot(x, up_buf[slot], preferred_element_type=jnp.float32)
        terms = g_buf[...]
        place = lax.broadcasted_iota(jnp.int32, terms.shape, 1) & 31
        share = jnp.sum(
            jnp.where(place == first + i // per_expert, terms, 0.0), axis=1, keepdims=True
        )
        act = gate / (1.0 + jnp.exp(-gate)) * up * share
        act_buf[:, pl.ds(pl.multiple_of(i * tile, tile), tile)] = act.astype(jnp.bfloat16)

        @pl.when(i + slots < steps)
        def _():
            for copy in fetch(i + slots):
                copy.start()

    def to_partner(c):
        return pltpu.make_async_remote_copy(
            src_ref=half_out.at[c],
            dst_ref=half_in.at[c],
            send_sem=half_sem.at[0, c],
            recv_sem=half_sem.at[1, c],
            device_id=partner,
            device_id_type=mesh_id,
        )

    def multiply(c):
        slot = lax.rem(c, down_slots)
        fetch_down(c).wait()
        y = jnp.dot(act_buf[...], down_buf[slot], preferred_element_type=jnp.float32)
        y_buf[lax.rem(c, 2)] = y.reshape(2, n * seqs, block)
        half_out[c] = y_buf[lax.rem(c, 2), 1 - side].astype(jnp.bfloat16)
        to_partner(c).start()

        @pl.when(c + down_slots < blocks)
        def _():
            fetch_down(c + down_slots).start()

    def spread(c):
        to_partner(c).wait_recv()
        total = y_buf[lax.rem(c, 2), side] + half_in[c].astype(jnp.float32)
        total = total.reshape(n, seqs, block)
        z_out[c] = jnp.concatenate(
            [total[:, :, : block // 2], total[:, :, block // 2 :]], axis=1
        ).astype(jnp.bfloat16)

        @pl.loop(1, n)
        def _(k):
            to = lax.rem(me + k, n)
            pltpu.make_async_remote_copy(
                src_ref=z_out.at[c, to],
                dst_ref=z_in.at[c, k - 1],
                send_sem=z_sem.at[0, c],
                recv_sem=z_sem.at[1, c],
                device_id={"dev": to},
                device_id_type=mesh_id,
            ).start()

    multiply(0)

    @pl.loop(1, blocks)
    def _(c):
        multiply(c)
        spread(c - 1)

    spread(blocks - 1)

    @pl.loop(0, blocks)
    def _(c):
        pltpu.make_async_copy(z_in.at[c], z_in.at[c], z_sem.at[1, c]).wait()
        total = jnp.sum(z_in[c].astype(jnp.float32), axis=0) + z_out[c, me].astype(jnp.float32)
        merged = jnp.concatenate([total[:seqs], total[seqs:]], axis=1)
        moe_ref[:, pl.ds(pl.multiple_of(c * block, block), block)] = merged.astype(jnp.bfloat16)
        to_partner(c).wait_send()
        pltpu.make_async_copy(z_in.at[c], z_in.at[c], z_sem.at[0, c]).wait()


def on_device(
    queries,
    kv_cache,
    new_kv,
    lengths,
    page_table,
    hidden,
    norm_gain,
    route_ids,
    route_weights,
    gate_w,
    up_w,
    down_w,
):
    seqs, depth = hidden.shape
    positions = kv_cache.shape[0] * PAGE
    columns = gate_w.shape[1]
    units = min(columns, FF)
    n = lax.axis_size("dev")
    ranks = n // 2
    tokens = 2 * n * seqs
    tile = 256 if units % 256 == 0 else 128
    slots = min(columns // tile, 8)
    block = 512
    blocks = depth // block
    down_slots = min(blocks, 4)
    bf16 = jnp.bfloat16
    dma = pltpu.SemaphoreType.DMA
    vmem = pl.BlockSpec(memory_space=pltpu.VMEM)
    hbm = pl.BlockSpec(memory_space=pl.ANY)
    context, moe_out = pl.pallas_call(
        functools.partial(layer, n, tile, block),
        out_shape=(
            jax.ShapeDtypeStruct((seqs, HEADS * HEAD_DIM), bf16),
            jax.ShapeDtypeStruct((seqs, depth), bf16),
        ),
        in_specs=[vmem] * 3 + [pl.BlockSpec(memory_space=pltpu.SMEM)] + [vmem] * 5 + [hbm] * 3,
        out_specs=(vmem, vmem),
        scratch_shapes=[
            pltpu.VMEM((slots, depth, tile), bf16),
            pltpu.VMEM((slots, depth, tile), bf16),
            pltpu.VMEM((down_slots, columns, block), bf16),
            pltpu.VMEM((2 * n, 2 * seqs, depth // 2 + 128), bf16),
            pltpu.VMEM((tokens, depth), bf16),
            pltpu.VMEM((tokens, 128), jnp.float32),
            pltpu.VMEM((tokens, columns), bf16),
            pltpu.VMEM((2, 2, n * seqs, block), jnp.float32),
            pltpu.VMEM((blocks, n * seqs, block), bf16),
            pltpu.VMEM((blocks, n * seqs, block), bf16),
            pltpu.VMEM((blocks, n, 2 * seqs, block // 2), bf16),
            pltpu.VMEM((blocks, n - 1, 2 * seqs, block // 2), bf16),
            dma((slots,)),
            dma((slots,)),
            dma((down_slots,)),
            dma((5,)),
            dma((ranks,)),
            dma((2, blocks)),
            dma((2, blocks)),
        ],
        compiler_params=pltpu.CompilerParams(
            collective_id=0, has_side_effects=True, vmem_limit_bytes=60 << 20
        ),
        cost_estimate=pl.CostEstimate(
            flops=6 * tokens * depth * columns,
            bytes_accessed=6 * depth * columns,
            transcendentals=tokens * columns,
        ),
    )(
        queries,
        kv_cache.reshape(positions, -1),
        new_kv,
        lengths,
        page_table,
        hidden,
        norm_gain.reshape(1, depth),
        route_ids,
        route_weights,
        gate_w,
        up_w,
        down_w,
    )
    return (context, moe_out)


def solution(mesh):
    rows = P(("groups", "side", "dev"), None)
    placed = (
        rows,
        P(("groups", "side", "dev"), None, None),
        rows,
        P(("groups", "side", "dev")),
        rows,
        rows,
        P(),
        rows,
        rows,
        P(None, ("side", "dev")),
        P(None, ("side", "dev")),
        P(("side", "dev"), None),
    )
    return jax.shard_map(
        on_device, mesh=mesh, in_specs=placed, out_specs=(rows, rows), check_vma=False
    )
```
